32 devices in a mesh: kocc: 8 (over z, y), vrow: 4 (over x, core).
Axes of the slice: x: 2, y: 2, z: 4, core: 2. Of those that a mesh axis runs over, the one named last changes fastest.
Arguments:
- factors: bfloat16 [8, 16, 128, 1536], P('kocc', None, 'vrow'), may hold values from -0.1875 to 0.1875
- amps: bfloat16 [4, 8, 16, 128, 1024], P(None, 'kocc', None, None, 'vrow'), may hold values from -6 to 6
- eps_occ: float32 [8, 16], P('kocc'), may hold values from -1 to -0.3
- eps_vir: bfloat16 [8, 128], P('kocc'), may hold values from 0.099609375 to 1
- col_energy: float32 [1024], P('vrow'), may hold values from 0.2 to 1.5
- q_index: int32 [1], replicated, may hold values from 1 to 7
Outputs:
- sigma: bfloat16 [4, 8, 16, 128, 1024], P(None, 'kocc', None, None, 'vrow')
The draws below stay inside these ranges and needn't reach their ends.
All inputs are finite; a program needn't handle non-finite values.
Results may differ from the reference program's by a relative error of at most 0.015.
Values may be sent and summed in bfloat16 or wider, within the bound.
A program may use at most 128 MiB of HBM per device.

```python
import jax
import jax.numpy as jnp
from jax import lax

NO = 16
NV = 128
NAUX = 1536
ROOTS = 4
NK = 8
J = 1024


def block_scale(key, shape, shards, least, largest):
    def one(position, blocks):
        draws = jax.random.uniform(jax.random.fold_in(jax.random.fold_in(key, 6), position), (blocks,), jnp.float32, least / len(shards), largest / len(shards))
        return jnp.repeat(jnp.exp(draws), shape[position] // blocks).reshape((-1,) + (1,) * (len(shape) - position - 1))

    loudness = one(*shards[0])
    for cut in shards[1:]:
        loudness = loudness * one(*cut)
    return loudness


def centred(key, extent, deviation, bound, cuts=(), kind=jnp.bfloat16):
    entries = jax.random.normal(key, extent, jnp.float32) * deviation
    if len(cuts) > 0:
        entries = block_scale(key, extent, cuts, -0.22, 0.18) * entries
    return jnp.clip(entries, min=-bound, max=bound).astype(kind)


def setup_inputs(seed: int = 0) -> dict:
    key_of = jax.random.split(jax.random.key(seed), 7)
    factors = centred(key_of[0], (NK, NO, NV, NAUX), (NV * NK) ** -0.5, 0.1875, ((0, 8), (2, 4)))
    amps = centred(key_of[1], (ROOTS, NK, NO, NV, J), 1.0, 6.0, ((1, 8), (4, 4)))
    eps_occ = jnp.clip(-1.0 + 0.7 * jax.random.uniform(key_of[2], (NK, NO), jnp.float32) ** block_scale(key_of[2], (NK, NO), ((0, 8),), -0.2, 0.2), -1.0, -0.3)
    eps_vir = jnp.clip(0.099609375 + 0.9003906 * jax.random.uniform(key_of[3], (NK, NV), jnp.float32) ** block_scale(key_of[3], (NK, NV), ((0, 8),), -0.2, 0.2), 0.099609375, 1.0).astype(jnp.bfloat16)
    col_energy = jnp.clip(0.2 + 1.3 * jax.random.uniform(key_of[4], (J,), jnp.float32) ** block_scale(key_of[4], (J,), ((0, 4),), -0.2, 0.2), 0.2, 1.5)
    q_index = jax.random.randint(key_of[5], (1,), 1, NK).astype(jnp.int32)
    return dict(factors=factors, amps=amps, eps_occ=eps_occ, eps_vir=eps_vir, col_energy=col_energy, q_index=q_index)


def reference(factors, amps, eps_occ, eps_vir, col_energy, q_index):
    momenta = jnp.arange(NK, dtype=jnp.int32)
    source = jnp.mod(momenta - q_index[0], NK).astype(jnp.int32)
    shifted = factors[source]
    vir_shift = eps_vir[source]
    factor_rows = shifted.reshape(NK * NO * NV, NAUX)
    amp_rows = amps.reshape(ROOTS, NK * NO * NV, J)
    cycle = lax.map(lambda amp_block: jnp.dot(factor_rows.T, amp_block, preferred_element_type=jnp.float32), amp_rows)
    cycle_b = cycle.astype(jnp.bfloat16)

    def per_point(inputs):
        point_factor, point_vir, point_occ, point_amps = inputs
        cycle_part = jnp.einsum('np,rpj->rnj', point_factor.reshape(NO * NV, NAUX).astype(jnp.float32), cycle_b.astype(jnp.float32))
        cycle_part = cycle_part.reshape(ROOTS, NO, NV, J)
        energy_gap = point_vir.astype(jnp.float32)[None, :, None] - point_occ[:, None, None] + col_energy[None, None, :]
        return (cycle_part + energy_gap[None] * point_amps.astype(jnp.float32)).astype(jnp.bfloat16)

    result = lax.map(per_point, (shifted, vir_shift, eps_occ, jnp.moveaxis(amps, 1, 0)))
    return jnp.moveaxis(result, 0, 1)
```

```python
import functools

import jax
import jax.numpy as jnp
from jax import lax
from jax.experimental import pallas as pl
from jax.experimental.pallas import tpu as pltpu
from jax.sharding import PartitionSpec as P

MESH = pl.DeviceIdType.MESH


def kernel(nk, nv, n, fac, amp, row_gap, col_gap, out,
           held, amp_t, acc, part, from_y, sum_y, from_z, full,
           own_sem, gx_s, gx_r, gc_s, gc_r, gf_s, gf_r,
           ry_s, ry_r, rz_s, rz_r, az_s, az_r, ay_s, ay_r):
    nx, nz = nv // 2, nk // 2
    k, v = lax.axis_index("kocc"), lax.axis_index("vrow")
    y, z = lax.rem(k, 2), k // 2
    core, x = lax.rem(v, 2), v // 2
    width = held.shape[-1]
    roots, rows, cols = amp.shape
    half = part.shape[1] // 2
    piece = half // nz

    def at_vrow(target):
        return {"kocc": k, "vrow": target}

    def at_kocc(target):
        return {"kocc": target, "vrow": v}

    mate = at_vrow(x * 2 + 1 - core)
    y_mate = at_kocc(z * 2 + 1 - y)

    def x_to(t):
        return lax.rem(x + t, nx)

    def x_from(t):
        return lax.rem(x + nx - t, nx)

    def z_to(t):
        return lax.rem(z + t, nz)

    def z_from(t):
        return lax.rem(z + nz - t, nz)

    barrier = pltpu.get_barrier_semaphore()
    partners = [mate, y_mate]
    partners += [at_vrow(x_to(t) * 2 + core) for t in range(1, nx)]
    partners += [at_kocc(z_to(t) * 2 + y) for t in range(1, nz)]
    for partner in partners:
        pl.semaphore_signal(barrier, inc=1, device_id=partner, device_id_type=MESH)
    pl.semaphore_wait(barrier, len(partners))

    def remote(src, dst, send, recv, device):
        return pltpu.make_async_remote_copy(
            src_ref=src, dst_ref=dst, send_sem=send, recv_sem=recv,
            device_id=device, device_id_type=MESH)

    def mine(p):
        return fac.at[:, :, pl.ds(pl.multiple_of(p * width, width), width)]

    def own(p):
        return pltpu.make_async_copy(mine(p), held.at[p, :, v], own_sem.at[p])

    def gather_x(p, t):
        return remote(mine(p), held.at[p, :, v], gx_s.at[p, t - 1], gx_r.at[p, t - 1],
                      at_vrow(x_to(t) * 2 + core))

    def gather_core(p):
        return remote(mine(p), held.at[p, :, v], gc_s.at[p], gc_r.at[p], mate)

    def gather_forward(p, t):
        slot = held.at[p, :, x_from(t) * 2 + core]
        return remote(slot, slot, gf_s.at[p, t - 1], gf_r.at[p, t - 1], mate)

    def reduce_y(p):
        return remote(part.at[p, pl.ds((1 - y) * half, half)], from_y.at[p],
                      ry_s.at[p], ry_r.at[p], y_mate)

    def reduce_z(p, t):
        return remote(sum_y.at[p, pl.ds(z_to(t) * piece, piece)], from_z.at[p, t - 1],
                      rz_s.at[p, t - 1], rz_r.at[p, t - 1], at_kocc(z_to(t) * 2 + y))

    def gather_z(p, t):
        where = pl.ds(y * half + z * piece, piece)
        return remote(full.at[p, where], full.at[p, where],
                      az_s.at[p, t - 1], az_r.at[p, t - 1], at_kocc(z_to(t) * 2 + y))

    def gather_y(p):
        where = pl.ds(y * half, half)
        return remote(full.at[p, where], full.at[p, where], ay_s.at[p], ay_r.at[p], y_mate)

    def start_gather(p):
        for t in range(1, nx):
            gather_x(p, t).start()
        gather_core(p).start()
        own(p).start()

    def forward(p):
        for t in range(1, nx):
            gather_x(p, t).wait_recv()
            gather_forward(p, t).start()

    start_gather(0)
    start_gather(1)

    block = 256

    @pl.loop(0, roots * (rows // block))
    def _(i):
        r, b = i // (rows // block), lax.rem(i, rows // block)
        at = pl.ds(pl.multiple_of(b * block, block), block)
        tile = amp[r, at, :]
        amp_t[r, :, at] = tile.T
        gap = row_gap[at, :] + col_gap[...]
        acc[r, at, :] = gap * tile.astype(jnp.float32)

    forward(0)

    def step(s, carry):
        @pl.when(s + 2 < n)
        def _():
            start_gather(s + 2)

        @pl.when(s + 1 < n)
        def _():
            forward(s + 1)

        @pl.when(s < n)
        def _():
            own(s).wait()
            gather_core(s).wait_recv()
            for t in range(1, nx):
                gather_forward(s, t).wait_recv()

            @pl.loop(0, roots)
            def _(r):
                dot = jnp.dot(amp_t[r], held[s].reshape(rows, width),
                              preferred_element_type=jnp.float32)
                at = pl.ds(pl.multiple_of(r * cols, cols), cols)
                part[s, at, :] = dot.astype(part.dtype)
            reduce_y(s).start()

        p1 = s - 1

        @pl.when((p1 >= 0) & (p1 < n))
        def _():
            reduce_y(p1).wait_recv()

            @pl.loop(0, nz)
            def _(i):
                at = pl.ds(pl.multiple_of(i * piece, piece), piece)
                mine_at = pl.ds(pl.multiple_of(y * half + i * piece, piece), piece)
                total = part[p1, mine_at, :].astype(jnp.float32) + from_y[p1, at, :].astype(jnp.float32)
                sum_y[p1, at, :] = total.astype(sum_y.dtype)
            for t in range(1, nz):
                reduce_z(p1, t).start()

        p2 = s - 2

        @pl.when((p2 >= 0) & (p2 < n))
        def _():
            total = sum_y[p2, pl.ds(pl.multiple_of(z * piece, piece), piece), :].astype(jnp.float32)
            for t in range(1, nz):
                reduce_z(p2, t).wait_recv()
                total += from_z[p2, t - 1].astype(jnp.float32)
            full[p2, pl.ds(pl.multiple_of(y * half + z * piece, piece), piece), :] = total.astype(full.dtype)
            for t in range(1, nz):
                gather_z(p2, t).start()

        p3 = s - 3

        @pl.when((p3 >= 0) & (p3 < n))
        def _():
            for t in range(1, nz):
                gather_z(p3, t).wait_recv()
            gather_y(p3).start()

        p4 = s - 4

        @pl.when((p4 >= 0) & (p4 < n))
        def _():
            gather_y(p4).wait_recv()

            @pl.loop(0, roots)
            def _(r):
                at = pl.ds(pl.multiple_of(r * cols, cols), cols)
                acc[r] += lax.dot_general(
                    held[p4].reshape(rows, width), full[p4, at, :],
                    (((1,), (1,)), ((), ())), preferred_element_type=jnp.float32)

        return carry

    lax.fori_loop(0, n + 4, step, 0)

    @pl.loop(0, roots * (rows // block))
    def _(i):
        r, b = i // (rows // block), lax.rem(i, rows // block)
        at = pl.ds(pl.multiple_of(b * block, block), block)
        out[r, at, :] = acc[r, at, :].astype(out.dtype)

    def drain(p, carry):
        for t in range(1, nx):
            gather_x(p, t).wait_send()
            gather_forward(p, t).wait_send()
        gather_core(p).wait_send()
        reduce_y(p).wait_send()
        for t in range(1, nz):
            reduce_z(p, t).wait_send()
            gather_z(p, t).wait_send()
        gather_y(p).wait_send()
        return carry

    lax.fori_loop(0, n, drain, 0)


def chunk_width(aux):
    for width in (256, 128):
        if aux % width == 0:
            return width
    return aux


def combine(fac, amp, row_gap, col_gap):
    nk, nv = lax.axis_size("kocc"), lax.axis_size("vrow")
    outer, inner, aux = fac.shape
    roots, rows, cols = amp.shape
    width = chunk_width(aux)
    n = aux // width
    nx, nz = nv // 2, nk // 2
    half = roots * cols // 2
    dma = pltpu.SemaphoreType.DMA
    vmem = pl.BlockSpec(memory_space=pltpu.VMEM)
    bf = jnp.bfloat16
    return pl.pallas_call(
        functools.partial(kernel, nk, nv, n),
        out_shape=jax.ShapeDtypeStruct((roots, rows, cols), bf),
        in_specs=[pl.BlockSpec(memory_space=pl.ANY), vmem, vmem, vmem],
        out_specs=vmem,
        scratch_shapes=[
            pltpu.VMEM((n, outer, nv, inner, width), bf),
            pltpu.VMEM((roots, cols, rows), bf),
            pltpu.VMEM((roots, rows, cols), jnp.float32),
            pltpu.VMEM((n, 2 * half, width), bf),
            pltpu.VMEM((n, half, width), bf),
            pltpu.VMEM((n, half, width), bf),
            pltpu.VMEM((n, nz - 1, half // nz, width), bf),
            pltpu.VMEM((n, 2 * half, width), bf),
            dma((n,)),
            dma((n, nx - 1)), dma((n, nx - 1)),
            dma((n,)), dma((n,)),
            dma((n, nx - 1)), dma((n, nx - 1)),
            dma((n,)), dma((n,)),
            dma((n, nz - 1)), dma((n, nz - 1)),
            dma((n, nz - 1)), dma((n, nz - 1)),
            dma((n,)), dma((n,)),
        ],
        compiler_params=pltpu.CompilerParams(
            collective_id=0, has_side_effects=True, vmem_limit_bytes=60 * 1024 * 1024),
        cost_estimate=pl.CostEstimate(
            flops=4 * roots * rows * cols * aux,
            bytes_accessed=4 * roots * rows * cols + 2 * outer * inner * aux,
            transcendentals=0),
    )(fac, amp, row_gap, col_gap)


def shift(distance, nk, block):
    if distance == 0:
        return block
    return lax.ppermute(block, "kocc", [(i, (i + distance) % nk) for i in range(nk)])


def shards(factors, amps, eps_occ, eps_vir, col_energy, q_index):
    nk, nv = lax.axis_size("kocc"), lax.axis_size("vrow")
    shifted, vir_shift = lax.switch(
        q_index[0], [functools.partial(shift, d, nk) for d in range(nk)], (factors, eps_vir))
    fac = shifted[0]
    occ, share, aux = fac.shape
    amp = amps[:, 0]
    roots, _, vir, cols = amp.shape
    gap = vir_shift[0].astype(jnp.float32)[None, :] - eps_occ[0][:, None]
    natural = share % 16 == 0
    if not natural:
        fac = fac.reshape(1, occ * share, aux)
        amp = amp.reshape(roots, occ, nv, share, cols).swapaxes(1, 2)
        gap = gap.reshape(occ, nv, share).swapaxes(0, 1)
    out = combine(fac, amp.reshape(roots, occ * vir, cols), gap.reshape(occ * vir, 1), col_energy[None, :])
    if not natural:
        out = out.reshape(roots, nv, occ, share, cols).swapaxes(1, 2)
    return out.reshape(roots, 1, occ, vir, cols)


def solution(mesh):
    in_specs = (
        P("kocc", None, "vrow", None),
        P(None, "kocc", None, None, "vrow"),
        P("kocc", None),
        P("kocc", None),
        P("vrow"),
        P(),
    )
    out_specs = P(None, "kocc", None, None, "vrow")
    return jax.shard_map(shards, mesh=mesh, in_specs=in_specs, out_specs=out_specs, check_vma=False)
```

```python
import functools

import jax
import jax.numpy as jnp
from jax import lax
from jax.experimental import pallas as pl
from jax.experimental.pallas import tpu as pltpu
from jax.sharding import PartitionSpec as P

MESH = pl.DeviceIdType.MESH
AHEAD = 3


def kernel(nk, nv, n, distance, fac, vir, amp_in, occ_rows, pick, col_gap, out,
           held, vir_got, amp, amp_t, acc, part, came, full,
           amp_sem, vir_s, vir_r, sh_s, sh_r, gx_s, gx_r, gc_s, gc_r, gf_s, gf_r,
           rs_s, rs_r, ag_s, ag_r):
    nx, levels = nv // 2, (nk - 1).bit_length()
    k, v = lax.axis_index("kocc"), lax.axis_index("vrow")
    core, x = lax.rem(v, 2), v // 2
    width = held.shape[-1]
    roots, rows, cols = amp.shape
    total = part.shape[1]
    piece = total // nk

    def at_vrow(target):
        return {"kocc": k, "vrow": target}

    def at_kocc(target):
        return {"kocc": target, "vrow": v}

    bit = [lax.rem(k // (1 << l), 2) for l in range(levels)]
    partner = [at_kocc(k + (1 - 2 * bit[l]) * (1 << l)) for l in range(levels)]
    offset = [0]
    for l in range(levels):
        offset.append(offset[-1] + bit[l] * (total >> (l + 1)))
    mate = at_vrow(x * 2 + 1 - core)
    ahead = at_kocc(lax.rem(k + distance, nk))
    behind = at_kocc(lax.rem(k + nk - distance, nk))

    def x_to(t):
        return lax.rem(x + t, nx)

    def x_from(t):
        return lax.rem(x + nx - t, nx)

    copy = pltpu.make_async_copy(amp_in, amp, amp_sem)
    copy.start()

    barrier = pltpu.get_barrier_semaphore()
    partners = [ahead, behind, mate] + partner
    partners += [at_vrow(x_to(t) * 2 + core) for t in range(1, nx)]
    for device in partners:
        pl.semaphore_signal(barrier, inc=1, device_id=device, device_id_type=MESH)
    pl.semaphore_wait(barrier, len(partners))

    def remote(src, dst, send, recv, device):
        return pltpu.make_async_remote_copy(
            src_ref=src, dst_ref=dst, send_sem=send, recv_sem=recv,
            device_id=device, device_id_type=MESH)

    def shift(p):
        return remote(fac.at[:, :, pl.ds(pl.multiple_of(p * width, width), width)],
                      held.at[p, :, v], sh_s.at[p], sh_r.at[p], ahead)

    def gather_x(p, t):
        return remote(held.at[p, :, v], held.at[p, :, v], gx_s.at[p, t - 1], gx_r.at[p, t - 1],
                      at_vrow(x_to(t) * 2 + core))

    def gather_core(p):
        return remote(held.at[p, :, v], held.at[p, :, v], gc_s.at[p], gc_r.at[p], mate)

    def gather_forward(p, t):
        slot = held.at[p, :, x_from(t) * 2 + core]
        return remote(slot, slot, gf_s.at[p, t - 1], gf_r.at[p, t - 1], mate)

    def scatter(p, l):
        size = total >> (l + 1)
        return remote(part.at[p, pl.ds(pl.multiple_of(offset[l] + (1 - bit[l]) * size, piece), size)],
                      came.at[p, pl.ds(total - (total >> l), size)],
                      rs_s.at[p, l], rs_r.at[p, l], partner[l])

    def gather(p, l):
        where = pl.ds(pl.multiple_of(offset[l + 1], piece), total >> (l + 1))
        return remote(full.at[p, where], full.at[p, where],
                      ag_s.at[p, l], ag_r.at[p, l], partner[l])

    shift_vir = remote(vir, vir_got, vir_s, vir_r, ahead)
    for p in range(AHEAD):
        shift(p).start()
    shift_vir.start()

    block = 256
    copy.wait()

    @pl.loop(0, roots * (rows // block))
    def _(i):
        r, b = i // (rows // block), lax.rem(i, rows // block)
        at = pl.ds(pl.multiple_of(b * block, block), block)
        amp_t[r, :, at] = amp[r, at, :].T

    shift_vir.wait_recv()

    def spread(p):
        shift(p).wait_recv()
        for t in range(1, nx):
            gather_x(p, t).start()
        gather_core(p).start()

    def forward(p):
        for t in range(1, nx):
            gather_x(p, t).wait_recv()
            gather_forward(p, t).start()

    def energies(r):
        @pl.loop(0, rows // block)
        def _(b):
            at = pl.ds(pl.multiple_of(b * block, block), block)
            gap = jnp.dot(pick[at, :], vir_got[...], preferred_element_type=jnp.float32) - occ_rows[at, :]
            for h in range(0, cols, 128):
                acc[r, at, h:h + 128] = (gap + col_gap[:, h:h + 128]) * amp[r, at, h:h + 128].astype(jnp.float32)

    def cycle(p):
        gather_core(p).wait_recv()
        for t in range(1, nx):
            gather_forward(p, t).wait_recv()

        @pl.loop(0, roots)
        def _(r):
            dot = jnp.dot(amp_t[r], held[p].reshape(rows, width), preferred_element_type=jnp.float32)
            part[p, pl.ds(pl.multiple_of(r * cols, cols), cols), :] = dot.astype(part.dtype)
        scatter(p, 0).start()

    def reduce(p, l):
        scatter(p, l).wait_recv()
        last = l == levels - 1
        into = full if last else part

        @pl.loop(0, (total >> (l + 1)) // piece)
        def _(i):
            at = pl.ds(pl.multiple_of(offset[l + 1] + i * piece, piece), piece)
            new = pl.ds(pl.multiple_of(total - (total >> l) + i * piece, piece), piece)
            both = part[p, at, :].astype(jnp.float32) + came[p, new, :].astype(jnp.float32)
            into[p, at, :] = both.astype(part.dtype)
        if last:
            gather(p, l).start()
        else:
            scatter(p, l + 1).start()

    def regather(p, l):
        gather(p, l).wait_recv()
        gather(p, l - 1).start()

    def sigma(p):
        gather(p, 0).wait_recv()

        def product(r):
            return lax.dot_general(
                held[p].reshape(rows, width), full[p, pl.ds(pl.multiple_of(r * cols, cols), cols), :],
                (((1,), (1,)), ((), ())), preferred_element_type=jnp.float32)

        @pl.when(p < n - 1)
        def _():
            @pl.loop(0, roots)
            def _(r):
                acc[r] += product(r)

        @pl.when(p == n - 1)
        def _():
            @pl.loop(0, roots)
            def _(r):
                out[r] = (acc[r] + product(r)).astype(out.dtype)

    stages = [spread, forward, cycle]
    stages += [functools.partial(reduce, l=l) for l in range(levels)]
    stages += [functools.partial(regather, l=l) for l in range(levels - 1, 0, -1)]
    stages += [sigma]

    def step(s, carry):
        @pl.when(s + AHEAD < n)
        def _():
            shift(s + AHEAD).start()

        for delay, stage in enumerate(stages):
            p = s - delay

            @pl.when((p >= 0) & (p < n))
            def _():
                stage(p)

            if delay == 0:
                @pl.when(s < roots)
                def _():
                    energies(s)

        return carry

    lax.fori_loop(0, n + len(stages) - 1, step, 0)

    def drain(p, carry):
        shift(p).wait_send()
        for t in range(1, nx):
            gather_x(p, t).wait_send()
            gather_forward(p, t).wait_send()
        gather_core(p).wait_send()
        for l in range(levels):
            scatter(p, l).wait_send()
            gather(p, l).wait_send()
        return carry

    lax.fori_loop(0, n, drain, 0)
    shift_vir.wait_send()


def combine(distance, nk, nv, fac, vir, amp, occ_rows, pick, col_gap):
    outer, inner, aux = fac.shape
    roots, rows, cols = amp.shape
    width = 128
    n = aux // width
    nx, levels = nv // 2, (nk - 1).bit_length()
    total = roots * cols
    dma = pltpu.SemaphoreType.DMA
    vmem = pl.BlockSpec(memory_space=pltpu.VMEM)
    anywhere = pl.BlockSpec(memory_space=pl.ANY)
    bf = jnp.bfloat16
    return pl.pallas_call(
        functools.partial(kernel, nk, nv, n, distance),
        out_shape=jax.ShapeDtypeStruct((roots, rows, cols), bf),
        in_specs=[anywhere, vmem, anywhere, vmem, vmem, vmem],
        out_specs=vmem,
        scratch_shapes=[
            pltpu.VMEM((n, outer, nv, inner, width), bf),
            pltpu.VMEM(vir.shape, bf),
            pltpu.VMEM((roots, rows, cols), bf),
            pltpu.VMEM((roots, cols, rows), bf),
            pltpu.VMEM((roots, rows, cols), jnp.float32),
            pltpu.VMEM((n, total, width), bf),
            pltpu.VMEM((n, total, width), bf),
            pltpu.VMEM((n, total, width), bf),
            dma, dma, dma,
            dma((n,)), dma((n,)),
            dma((n, nx - 1)), dma((n, nx - 1)),
            dma((n,)), dma((n,)),
            dma((n, nx - 1)), dma((n, nx - 1)),
            dma((n, levels)), dma((n, levels)),
            dma((n, levels)), dma((n, levels)),
        ],
        compiler_params=pltpu.CompilerParams(
            collective_id=distance, has_side_effects=True, vmem_limit_bytes=60 * 1024 * 1024),
        cost_estimate=pl.CostEstimate(
            flops=4 * roots * rows * cols * aux,
            bytes_accessed=4 * roots * rows * cols + 2 * outer * inner * aux,
            transcendentals=0),
    )(fac, vir, amp, occ_rows, pick, col_gap)


def shards(factors, amps, eps_occ, eps_vir, col_energy, q_index):
    nk, nv = lax.axis_size("kocc"), lax.axis_size("vrow")
    fac = factors[0]
    occ, share, aux = fac.shape
    amp = amps[:, 0]
    roots, _, vir, cols = amp.shape
    lanes = 128
    occ_rows = jnp.broadcast_to(eps_occ[0][:, None, None], (occ, vir, lanes))
    pick = jnp.broadcast_to(jnp.eye(vir, dtype=jnp.bfloat16), (occ, vir, vir))
    vir_lanes = jnp.broadcast_to(eps_vir[0][:, None], (vir, lanes))
    natural = share % 16 == 0
    if not natural:
        fac = fac.reshape(1, occ * share, aux)
        amp = amp.reshape(roots, occ, nv, share, cols).swapaxes(1, 2)
        occ_rows = occ_rows.reshape(occ, nv, share, lanes).swapaxes(0, 1)
        pick = pick.reshape(occ, nv, share, vir).swapaxes(0, 1)
    rows = occ * vir
    operands = (fac, vir_lanes, amp.reshape(roots, rows, cols), occ_rows.reshape(rows, lanes),
                pick.reshape(rows, vir), col_energy[None, :])
    out = lax.switch(
        q_index[0] - 1, [functools.partial(combine, d, nk, nv) for d in range(1, nk)], *operands)
    if not natural:
        out = out.reshape(roots, nv, occ, share, cols).swapaxes(1, 2)
    return out.reshape(roots, 1, occ, vir, cols)


def solution(mesh):
    in_specs = (
        P("kocc", None, "vrow", None),
        P(None, "kocc", None, None, "vrow"),
        P("kocc", None),
        P("kocc", None),
        P("vrow"),
        P(),
    )
    out_specs = P(None, "kocc", None, None, "vrow")
    return jax.shard_map(shards, mesh=mesh, in_specs=in_specs, out_specs=out_specs, check_vma=False)
```

```python
import functools

import jax
import jax.numpy as jnp
from jax import lax
from jax.experimental import pallas as pl
from jax.experimental.pallas import tpu as pltpu
from jax.sharding import PartitionSpec as P

MESH = pl.DeviceIdType.MESH
AHEAD = 3


def kernel(nk, nv, n, distance, fac, vir, amp_in, occ, col_gap, out,
           held, vir_put, vir_got, row_gap, amp, amp_t, acc, part, came, full,
           amp_sem, out_sem, vir_s, vir_r, sh_s, sh_r, gx_s, gx_r, gc_s, gc_r, gf_s, gf_r,
           rs_s, rs_r, ag_s, ag_r):
    nx, levels = nv // 2, (nk - 1).bit_length()
    k, v = lax.axis_index("kocc"), lax.axis_index("vrow")
    core, x = lax.rem(v, 2), v // 2
    width = held.shape[-1]
    roots, rows, cols = amp.shape
    total = part.shape[1]
    piece = total // nk

    def at_vrow(target):
        return {"kocc": k, "vrow": target}

    def at_kocc(target):
        return {"kocc": target, "vrow": v}

    bit = [lax.rem(k // (1 << l), 2) for l in range(levels)]
    partner = [at_kocc(k + (1 - 2 * bit[l]) * (1 << l)) for l in range(levels)]
    offset = [0]
    for l in range(levels):
        offset.append(offset[-1] + bit[l] * (total >> (l + 1)))
    mate = at_vrow(x * 2 + 1 - core)
    ahead = at_kocc(lax.rem(k + distance, nk))
    behind = at_kocc(lax.rem(k + nk - distance, nk))

    def x_to(t):
        return lax.rem(x + t, nx)

    def x_from(t):
        return lax.rem(x + nx - t, nx)

    copy = pltpu.make_async_copy(amp_in, amp, amp_sem)
    copy.start()

    barrier = pltpu.get_barrier_semaphore()
    partners = [ahead, behind, mate] + partner
    partners += [at_vrow(x_to(t) * 2 + core) for t in range(1, nx)]
    for device in partners:
        pl.semaphore_signal(barrier, inc=1, device_id=device, device_id_type=MESH)
    pl.semaphore_wait(barrier, len(partners))

    def remote(src, dst, send, recv, device):
        return pltpu.make_async_remote_copy(
            src_ref=src, dst_ref=dst, send_sem=send, recv_sem=recv,
            device_id=device, device_id_type=MESH)

    def shift(p):
        return remote(fac.at[:, :, pl.ds(pl.multiple_of(p * width, width), width)],
                      held.at[p, :, v], sh_s.at[p], sh_r.at[p], ahead)

    def gather_x(p, t):
        return remote(held.at[p, :, v], held.at[p, :, v], gx_s.at[p, t - 1], gx_r.at[p, t - 1],
                      at_vrow(x_to(t) * 2 + core))

    def gather_core(p):
        return remote(held.at[p, :, v], held.at[p, :, v], gc_s.at[p], gc_r.at[p], mate)

    def gather_forward(p, t):
        slot = held.at[p, :, x_from(t) * 2 + core]
        return remote(slot, slot, gf_s.at[p, t - 1], gf_r.at[p, t - 1], mate)

    def scatter(p, l):
        size = total >> (l + 1)
        return remote(part.at[p, pl.ds(pl.multiple_of(offset[l] + (1 - bit[l]) * size, piece), size)],
                      came.at[p, pl.ds(total - (total >> l), size)],
                      rs_s.at[p, l], rs_r.at[p, l], partner[l])

    def gather(p, l):
        where = pl.ds(pl.multiple_of(offset[l + 1], piece), total >> (l + 1))
        return remote(full.at[p, where], full.at[p, where],
                      ag_s.at[p, l], ag_r.at[p, l], partner[l])

    for p in range(AHEAD):
        shift(p).start()
    vir_put[...] = jnp.broadcast_to(vir[...].astype(jnp.float32), vir_put.shape).astype(vir_put.dtype)
    shift_vir = remote(vir_put, vir_got, vir_s, vir_r, ahead)
    shift_vir.start()

    block = 256
    copy.wait()

    @pl.loop(0, roots * (rows // block))
    def _(i):
        r, b = i // (rows // block), lax.rem(i, rows // block)
        at = pl.ds(pl.multiple_of(b * block, block), block)
        amp_t[r, :, at] = amp[r, at, :].T

    shift_vir.wait_recv()

    occs, virs = occ.shape[1], vir.shape[1]
    share = virs // nv

    def split(value, by):
        by = jnp.full_like(value, by)
        return lax.div(value, by), lax.rem(value, by)

    def chosen(values, index):
        lane = lax.broadcasted_iota(jnp.int32, (block, values.shape[1]), 1)
        return jnp.sum(jnp.where(lane == index, values, 0.0), axis=1, keepdims=True)

    @pl.loop(0, rows // block)
    def _(b):
        row = b * block + lax.broadcasted_iota(jnp.int32, (block, 1), 0)
        if held.shape[1] > 1:
            i, a = split(row, virs)
        else:
            owner, rest = split(row, occs * share)
            i, a = split(rest, share)
            a += owner * share
        got = vir_got[...].astype(jnp.float32)[0:1, :]
        gap = chosen(got, a) - chosen(occ[...], i)
        at = pl.ds(pl.multiple_of(b * block, block), block)
        row_gap[at, :] = jnp.broadcast_to(gap, (block, row_gap.shape[1]))

    def spread(p):
        shift(p).wait_recv()
        for t in range(1, nx):
            gather_x(p, t).start()
        gather_core(p).start()

    def forward(p):
        for t in range(1, nx):
            gather_x(p, t).wait_recv()
            gather_forward(p, t).start()

    def energies(r):
        @pl.loop(0, rows // block)
        def _(b):
            at = pl.ds(pl.multiple_of(b * block, block), block)
            gap = row_gap[at, :]
            for h in range(0, cols, 128):
                acc[r, at, h:h + 128] = (gap + col_gap[:, h:h + 128]) * amp[r, at, h:h + 128].astype(jnp.float32)

    def cycle(p):
        gather_core(p).wait_recv()
        for t in range(1, nx):
            gather_forward(p, t).wait_recv()

        @pl.loop(0, roots)
        def _(r):
            dot = jnp.dot(amp_t[r], held[p].reshape(rows, width), preferred_element_type=jnp.float32)
            part[p, pl.ds(pl.multiple_of(r * cols, cols), cols), :] = dot.astype(part.dtype)
        scatter(p, 0).start()

    def reduce(p, l):
        scatter(p, l).wait_recv()
        last = l == levels - 1
        into = full if last else part

        @pl.loop(0, (total >> (l + 1)) // piece)
        def _(i):
            at = pl.ds(pl.multiple_of(offset[l + 1] + i * piece, piece), piece)
            new = pl.ds(pl.multiple_of(total - (total >> l) + i * piece, piece), piece)
            both = part[p, at, :].astype(jnp.float32) + came[p, new, :].astype(jnp.float32)
            into[p, at, :] = both.astype(part.dtype)
        if last:
            gather(p, l).start()
        else:
            scatter(p, l + 1).start()

    def regather(p, l):
        gather(p, l).wait_recv()
        gather(p, l - 1).start()

    def deliver(r):
        return pltpu.make_async_copy(amp.at[r], out.at[r], out_sem.at[r])

    def sigma(p):
        gather(p, 0).wait_recv()

        def product(r):
            return lax.dot_general(
                held[p].reshape(rows, width), full[p, pl.ds(pl.multiple_of(r * cols, cols), cols), :],
                (((1,), (1,)), ((), ())), preferred_element_type=jnp.float32)

        @pl.when(p < n - 1)
        def _():
            @pl.loop(0, roots)
            def _(r):
                acc[r] += product(r)

        @pl.when(p == n - 1)
        def _():
            @pl.loop(0, roots)
            def _(r):
                amp[r] = (acc[r] + product(r)).astype(amp.dtype)
                deliver(r).start()

    stages, late = [(0, spread), (2, forward)], [(3, cycle)]
    delay = 3
    for l in range(levels):
        delay += 2
        stages.append((delay, functools.partial(reduce, l=l)))
    for l in range(levels - 1, 0, -1):
        delay += 2
        stages.append((delay, functools.partial(regather, l=l)))
    delay += 2
    late.append((delay, sigma))

    def step(s, carry):
        @pl.when(s + AHEAD < n)
        def _():
            shift(s + AHEAD).start()

        for behind_by, stage in stages + late:
            p = s - behind_by

            @pl.when((p >= 0) & (p < n))
            def _():
                stage(p)

        @pl.when(s < roots)
        def _():
            energies(s)

        return carry

    lax.fori_loop(0, n + delay, step, 0)

    def drain(p, carry):
        shift(p).wait_send()
        for t in range(1, nx):
            gather_x(p, t).wait_send()
            gather_forward(p, t).wait_send()
        gather_core(p).wait_send()
        for l in range(levels):
            scatter(p, l).wait_send()
            gather(p, l).wait_send()
        return carry

    lax.fori_loop(0, n, drain, 0)
    shift_vir.wait_send()
    for r in range(roots):
        deliver(r).wait()


def combine(distance, nk, nv, fac, vir, amp, occ, col_gap):
    outer, inner, aux = fac.shape
    roots, rows, cols = amp.shape
    width = 128
    n = aux // width
    nx, levels = nv // 2, (nk - 1).bit_length()
    total = roots * cols
    dma = pltpu.SemaphoreType.DMA
    vmem = pl.BlockSpec(memory_space=pltpu.VMEM)
    anywhere = pl.BlockSpec(memory_space=pl.ANY)
    bf = jnp.bfloat16
    return pl.pallas_call(
        functools.partial(kernel, nk, nv, n, distance),
        out_shape=jax.ShapeDtypeStruct((roots, rows, cols), bf),
        in_specs=[anywhere, vmem, anywhere, vmem, vmem],
        out_specs=anywhere,
        scratch_shapes=[
            pltpu.VMEM((n, outer, nv, inner, width), bf),
            pltpu.VMEM((16, vir.shape[1]), bf),
            pltpu.VMEM((16, vir.shape[1]), bf),
            pltpu.VMEM((rows, 128), jnp.float32),
            pltpu.VMEM((roots, rows, cols), bf),
            pltpu.VMEM((roots, cols, rows), bf),
            pltpu.VMEM((roots, rows, cols), jnp.float32),
            pltpu.VMEM((n, total, width), bf),
            pltpu.VMEM((n, total, width), bf),
            pltpu.VMEM((n, total, width), bf),
            dma, dma((roots,)), dma, dma,
            dma((n,)), dma((n,)),
            dma((n, nx - 1)), dma((n, nx - 1)),
            dma((n,)), dma((n,)),
            dma((n, nx - 1)), dma((n, nx - 1)),
            dma((n, levels)), dma((n, levels)),
            dma((n, levels)), dma((n, levels)),
        ],
        compiler_params=pltpu.CompilerParams(
            collective_id=distance, has_side_effects=True, vmem_limit_bytes=60 * 1024 * 1024),
        cost_estimate=pl.CostEstimate(
            flops=4 * roots * rows * cols * aux,
            bytes_accessed=4 * roots * rows * cols + 2 * outer * inner * aux,
            transcendentals=0),
    )(fac, vir, amp, occ, col_gap)


def shards(factors, amps, eps_occ, eps_vir, col_energy, q_index):
    nk, nv = lax.axis_size("kocc"), lax.axis_size("vrow")
    fac = factors[0]
    occ, share, aux = fac.shape
    amp = amps[:, 0]
    roots, _, vir, cols = amp.shape
    natural = share % 16 == 0
    if not natural:
        fac = fac.reshape(1, occ * share, aux)
        amp = amp.reshape(roots, occ, nv, share, cols).swapaxes(1, 2)
    operands = (fac, eps_vir, amp.reshape(roots, occ * vir, cols), eps_occ, col_energy[None, :])
    out = lax.switch(
        q_index[0] - 1, [functools.partial(combine, d, nk, nv) for d in range(1, nk)], *operands)
    if not natural:
        out = out.reshape(roots, nv, occ, share, cols).swapaxes(1, 2)
    return out.reshape(roots, 1, occ, vir, cols)


def solution(mesh):
    in_specs = (
        P("kocc", None, "vrow", None),
        P(None, "kocc", None, None, "vrow"),
        P("kocc", None),
        P("kocc", None),
        P("vrow"),
        P(),
    )
    out_specs = P(None, "kocc", None, None, "vrow")
    return jax.shard_map(shards, mesh=mesh, in_specs=in_specs, out_specs=out_specs, check_vma=False)
```

```python
import functools

import jax
import jax.numpy as jnp
from jax import lax
from jax.experimental import pallas as pl
from jax.experimental.pallas import tpu as pltpu
from jax.sharding import PartitionSpec as P

MESH = pl.DeviceIdType.MESH
AHEAD = 2


def kernel(nk, nv, n, distance, fac, vir, amp_in, occ, col_gap, out,
           held, vir_put, vir_got, row_gap, amp, amp_t, acc, part, came, full,
           amp_sem, out_sem, vir_s, vir_r, sh_s, sh_r, gx_s, gx_r, gc_s, gc_r, gf_s, gf_r,
           rs_s, rs_r, ag_s, ag_r):
    nx, levels = nv // 2, (nk - 1).bit_length()
    k, v = lax.axis_index("kocc"), lax.axis_index("vrow")
    core, x = lax.rem(v, 2), v // 2
    width = held.shape[-1]
    roots, rows, cols = amp.shape
    total = part.shape[1]
    piece = total // nk

    def at_vrow(target):
        return {"kocc": k, "vrow": target}

    def at_kocc(target):
        return {"kocc": target, "vrow": v}

    bit = [lax.rem(k // (1 << l), 2) for l in range(levels)]
    partner = [at_kocc(k + (1 - 2 * bit[l]) * (1 << l)) for l in range(levels)]
    offset = [0]
    for l in range(levels):
        offset.append(offset[-1] + bit[l] * (total >> (l + 1)))
    mate = at_vrow(x * 2 + 1 - core)
    ahead = at_kocc(lax.rem(k + distance, nk))
    behind = at_kocc(lax.rem(k + nk - distance, nk))

    def x_to(t):
        return lax.rem(x + t, nx)

    def x_from(t):
        return lax.rem(x + nx - t, nx)

    copy = pltpu.make_async_copy(amp_in, amp, amp_sem)
    copy.start()

    barrier = pltpu.get_barrier_semaphore()
    partners = [ahead, behind, mate] + partner
    partners += [at_vrow(x_to(t) * 2 + core) for t in range(1, nx)]
    for device in partners:
        pl.semaphore_signal(barrier, inc=1, device_id=device, device_id_type=MESH)
    pl.semaphore_wait(barrier, len(partners))

    def remote(src, dst, send, recv, device):
        return pltpu.make_async_remote_copy(
            src_ref=src, dst_ref=dst, send_sem=send, recv_sem=recv,
            device_id=device, device_id_type=MESH)

    def shift(p):
        return remote(fac.at[:, :, pl.ds(pl.multiple_of(p * width, width), width)],
                      held.at[p, :, v], sh_s.at[p], sh_r.at[p], ahead)

    def gather_x(p, t):
        return remote(held.at[p, :, v], held.at[p, :, v], gx_s.at[p, t - 1], gx_r.at[p, t - 1],
                      at_vrow(x_to(t) * 2 + core))

    def gather_core(p):
        return remote(held.at[p, :, v], held.at[p, :, v], gc_s.at[p], gc_r.at[p], mate)

    def gather_forward(p, t):
        slot = held.at[p, :, x_from(t) * 2 + core]
        return remote(slot, slot, gf_s.at[p, t - 1], gf_r.at[p, t - 1], mate)

    def scatter(p, l):
        size = total >> (l + 1)
        return remote(part.at[p, pl.ds(pl.multiple_of(offset[l] + (1 - bit[l]) * size, piece), size)],
                      came.at[p, pl.ds(total - (total >> l), size)],
                      rs_s.at[p, l], rs_r.at[p, l], partner[l])

    def gather(p, l):
        where = pl.ds(pl.multiple_of(offset[l + 1], piece), total >> (l + 1))
        return remote(full.at[p, where], full.at[p, where],
                      ag_s.at[p, l], ag_r.at[p, l], partner[l])

    for p in range(AHEAD):
        shift(p).start()
    vir_put[...] = jnp.broadcast_to(vir[...].astype(jnp.float32), vir_put.shape).astype(vir_put.dtype)
    shift_vir = remote(vir_put, vir_got, vir_s, vir_r, ahead)
    shift_vir.start()

    block = 256
    copy.wait()

    @pl.loop(0, roots * (rows // block))
    def _(i):
        r, b = i // (rows // block), lax.rem(i, rows // block)
        at = pl.ds(pl.multiple_of(b * block, block), block)
        amp_t[r, :, at] = amp[r, at, :].T

    shift_vir.wait_recv()

    occs, virs = occ.shape[1], vir.shape[1]
    share = virs // nv

    def split(value, by):
        by = jnp.full_like(value, by)
        return lax.div(value, by), lax.rem(value, by)

    def chosen(values, index):
        lane = lax.broadcasted_iota(jnp.int32, (block, values.shape[1]), 1)
        return jnp.sum(jnp.where(lane == index, values, 0.0), axis=1, keepdims=True)

    @pl.loop(0, rows // block)
    def _(b):
        row = b * block + lax.broadcasted_iota(jnp.int32, (block, 1), 0)
        if held.shape[1] > 1:
            i, a = split(row, virs)
        else:
            owner, rest = split(row, occs * share)
            i, a = split(rest, share)
            a += owner * share
        got = vir_got[...].astype(jnp.float32)[0:1, :]
        gap = chosen(got, a) - chosen(occ[...], i)
        at = pl.ds(pl.multiple_of(b * block, block), block)
        row_gap[at, :] = jnp.broadcast_to(gap, (block, row_gap.shape[1]))

    def spread(p):
        shift(p).wait_recv()
        for t in range(1, nx):
            gather_x(p, t).start()
        gather_core(p).start()

    def forward(p):
        for t in range(1, nx):
            gather_x(p, t).wait_recv()
            gather_forward(p, t).start()

    def energies(r):
        @pl.loop(0, rows // block)
        def _(b):
            at = pl.ds(pl.multiple_of(b * block, block), block)
            gap = row_gap[at, :]
            for h in range(0, cols, 128):
                acc[r, at, h:h + 128] = (gap + col_gap[:, h:h + 128]) * amp[r, at, h:h + 128].astype(jnp.float32)

    def cycle(p):
        gather_core(p).wait_recv()
        for t in range(1, nx):
            gather_forward(p, t).wait_recv()

        @pl.loop(0, roots)
        def _(r):
            dot = jnp.dot(amp_t[r], held[p].reshape(rows, width), preferred_element_type=jnp.float32)
            part[p, pl.ds(pl.multiple_of(r * cols, cols), cols), :] = dot.astype(part.dtype)
        scatter(p, 0).start()

    def reduce(p, l):
        scatter(p, l).wait_recv()
        last = l == levels - 1
        into = full if last else part

        @pl.loop(0, (total >> (l + 1)) // piece)
        def _(i):
            at = pl.ds(pl.multiple_of(offset[l + 1] + i * piece, piece), piece)
            new = pl.ds(pl.multiple_of(total - (total >> l) + i * piece, piece), piece)
            both = part[p, at, :].astype(jnp.float32) + came[p, new, :].astype(jnp.float32)
            into[p, at, :] = both.astype(part.dtype)
        if last:
            gather(p, l).start()
        else:
            scatter(p, l + 1).start()

    def regather(p, l):
        gather(p, l).wait_recv()
        gather(p, l - 1).start()

    def deliver(r):
        return pltpu.make_async_copy(amp.at[r], out.at[r], out_sem.at[r])

    def sigma(p):
        gather(p, 0).wait_recv()

        def product(r):
            return lax.dot_general(
                held[p].reshape(rows, width), full[p, pl.ds(pl.multiple_of(r * cols, cols), cols), :],
                (((1,), (1,)), ((), ())), preferred_element_type=jnp.float32)

        @pl.when(p < n - 1)
        def _():
            @pl.loop(0, roots)
            def _(r):
                acc[r] += product(r)

        @pl.when(p == n - 1)
        def _():
            @pl.loop(0, roots)
            def _(r):
                amp[r] = (acc[r] + product(r)).astype(amp.dtype)
                deliver(r).start()

    fill = [[(1, cycle)], [(0, forward), (4, sigma)]]
    stages = [(0, spread)]
    for l in range(levels):
        stages.append((2, functools.partial(reduce, l=l)))
        if l < levels - 1:
            stages.append((3, functools.partial(regather, l=levels - 1 - l)))
            if fill:
                stages += fill.pop(0)
    for rest in fill:
        stages += rest

    def step(s, carry):
        @pl.when(s + AHEAD < n)
        def _():
            shift(s + AHEAD).start()

        for behind_by, stage in stages:
            p = s - behind_by

            @pl.when((p >= 0) & (p < n))
            def _():
                stage(p)

        @pl.when(s < roots)
        def _():
            energies(s)

        return carry

    lax.fori_loop(0, n + 4, step, 0)

    def drain(p, carry):
        shift(p).wait_send()
        for t in range(1, nx):
            gather_x(p, t).wait_send()
            gather_forward(p, t).wait_send()
        gather_core(p).wait_send()
        for l in range(levels):
            scatter(p, l).wait_send()
            gather(p, l).wait_send()
        return carry

    lax.fori_loop(0, n, drain, 0)
    shift_vir.wait_send()
    for r in range(roots):
        deliver(r).wait()


def combine(distance, nk, nv, fac, vir, amp, occ, col_gap):
    outer, inner, aux = fac.shape
    roots, rows, cols = amp.shape
    width = 128
    n = aux // width
    nx, levels = nv // 2, (nk - 1).bit_length()
    total = roots * cols
    dma = pltpu.SemaphoreType.DMA
    vmem = pl.BlockSpec(memory_space=pltpu.VMEM)
    anywhere = pl.BlockSpec(memory_space=pl.ANY)
    bf = jnp.bfloat16
    return pl.pallas_call(
        functools.partial(kernel, nk, nv, n, distance),
        out_shape=jax.ShapeDtypeStruct((roots, rows, cols), bf),
        in_specs=[anywhere, vmem, anywhere, vmem, vmem],
        out_specs=anywhere,
        scratch_shapes=[
            pltpu.VMEM((n, outer, nv, inner, width), bf),
            pltpu.VMEM((16, vir.shape[1]), bf),
            pltpu.VMEM((16, vir.shape[1]), bf),
            pltpu.VMEM((rows, 128), jnp.float32),
            pltpu.VMEM((roots, rows, cols), bf),
            pltpu.VMEM((roots, cols, rows), bf),
            pltpu.VMEM((roots, rows, cols), jnp.float32),
            pltpu.VMEM((n, total, width), bf),
            pltpu.VMEM((n, total, width), bf),
            pltpu.VMEM((n, total, width), bf),
            dma, dma((roots,)), dma, dma,
            dma((n,)), dma((n,)),
            dma((n, nx - 1)), dma((n, nx - 1)),
            dma((n,)), dma((n,)),
            dma((n, nx - 1)), dma((n, nx - 1)),
            dma((n, levels)), dma((n, levels)),
            dma((n, levels)), dma((n, levels)),
        ],
        compiler_params=pltpu.CompilerParams(
            collective_id=distance, has_side_effects=True, vmem_limit_bytes=60 * 1024 * 1024),
        cost_estimate=pl.CostEstimate(
            flops=4 * roots * rows * cols * aux,
            bytes_accessed=4 * roots * rows * cols + 2 * outer * inner * aux,
            transcendentals=0),
    )(fac, vir, amp, occ, col_gap)


def shards(factors, amps, eps_occ, eps_vir, col_energy, q_index):
    nk, nv = lax.axis_size("kocc"), lax.axis_size("vrow")
    fac = factors[0]
    occ, share, aux = fac.shape
    amp = amps[:, 0]
    roots, _, vir, cols = amp.shape
    natural = share % 16 == 0
    if not natural:
        fac = fac.reshape(1, occ * share, aux)
        amp = amp.reshape(roots, occ, nv, share, cols).swapaxes(1, 2)
    operands = (fac, eps_vir, amp.reshape(roots, occ * vir, cols), eps_occ, col_energy[None, :])
    out = lax.switch(
        q_index[0] - 1, [functools.partial(combine, d, nk, nv) for d in range(1, nk)], *operands)
    if not natural:
        out = out.reshape(roots, nv, occ, share, cols).swapaxes(1, 2)
    return out.reshape(roots, 1, occ, vir, cols)


def solution(mesh):
    in_specs = (
        P("kocc", None, "vrow", None),
        P(None, "kocc", None, None, "vrow"),
        P("kocc", None),
        P("kocc", None),
        P("vrow"),
        P(),
    )
    out_specs = P(None, "kocc", None, None, "vrow")
    return jax.shard_map(shards, mesh=mesh, in_specs=in_specs, out_specs=out_specs, check_vma=False)
```

```python
import functools

import jax
import jax.numpy as jnp
from jax import lax
from jax.experimental import pallas as pl
from jax.experimental.pallas import tpu as pltpu
from jax.sharding import PartitionSpec as P

MESH = pl.DeviceIdType.MESH
AHEAD = 2


def kernel(nk, nv, n, distance, fac, vir, amp_in, occ, col_gap, out,
           held, vir_put, vir_got, row_gap, amp, amp_t, acc, part, came, full,
           amp_sem, out_sem, vir_s, vir_r, sh_s, sh_r, gx_s, gx_r, gc_s, gc_r, gf_s, gf_r,
           rs_s, rs_r, ag_s, ag_r):
    nx, levels = nv // 2, (nk - 1).bit_length()
    k, v = lax.axis_index("kocc"), lax.axis_index("vrow")
    core, x = lax.rem(v, 2), v // 2
    width = held.shape[-1]
    roots, rows, cols = amp.shape
    total = part.shape[1]
    piece = total // nk

    def at_vrow(target):
        return {"kocc": k, "vrow": target}

    def at_kocc(target):
        return {"kocc": target, "vrow": v}

    bit = [lax.rem(k // (1 << l), 2) for l in range(levels)]
    partner = [at_kocc(k + (1 - 2 * bit[l]) * (1 << l)) for l in range(levels)]
    offset = [0]
    for l in range(levels):
        offset.append(offset[-1] + bit[l] * (total >> (l + 1)))
    mate = at_vrow(x * 2 + 1 - core)
    ahead = at_kocc(lax.rem(k + distance, nk))
    behind = at_kocc(lax.rem(k + nk - distance, nk))

    def x_to(t):
        return lax.rem(x + t, nx)

    def x_from(t):
        return lax.rem(x + nx - t, nx)

    copy = pltpu.make_async_copy(amp_in, amp, amp_sem)
    copy.start()

    barrier = pltpu.get_barrier_semaphore()
    partners = [ahead, behind, mate] + partner
    partners += [at_vrow(x_to(t) * 2 + core) for t in range(1, nx)]
    for device in partners:
        pl.semaphore_signal(barrier, inc=1, device_id=device, device_id_type=MESH)
    pl.semaphore_wait(barrier, len(partners))

    def remote(src, dst, send, recv, device):
        return pltpu.make_async_remote_copy(
            src_ref=src, dst_ref=dst, send_sem=send, recv_sem=recv,
            device_id=device, device_id_type=MESH)

    def shift(p):
        return remote(fac.at[:, :, pl.ds(pl.multiple_of(p * width, width), width)],
                      held.at[p, :, v], sh_s.at[p], sh_r.at[p], ahead)

    def gather_x(p, t):
        return remote(held.at[p, :, v], held.at[p, :, v], gx_s.at[p, t - 1], gx_r.at[p, t - 1],
                      at_vrow(x_to(t) * 2 + core))

    def gather_core(p):
        return remote(held.at[p, :, v], held.at[p, :, v], gc_s.at[p], gc_r.at[p], mate)

    def gather_forward(p, t):
        slot = held.at[p, :, x_from(t) * 2 + core]
        return remote(slot, slot, gf_s.at[p, t - 1], gf_r.at[p, t - 1], mate)

    def scatter(p, l):
        size = total >> (l + 1)
        return remote(part.at[p, pl.ds(pl.multiple_of(offset[l] + (1 - bit[l]) * size, piece), size)],
                      came.at[p, pl.ds(total - (total >> l), size)],
                      rs_s.at[p, l], rs_r.at[p, l], partner[l])

    def gather(p, l):
        where = pl.ds(pl.multiple_of(offset[l + 1], piece), total >> (l + 1))
        return remote(full.at[p, where], full.at[p, where],
                      ag_s.at[p, l], ag_r.at[p, l], partner[l])

    for p in range(AHEAD):
        shift(p).start()
    vir_put[...] = jnp.broadcast_to(vir[...].astype(jnp.float32), vir_put.shape).astype(vir_put.dtype)
    shift_vir = remote(vir_put, vir_got, vir_s, vir_r, ahead)
    shift_vir.start()

    block = 256
    copy.wait()

    @pl.loop(0, roots * (rows // block))
    def _(i):
        r, b = i // (rows // block), lax.rem(i, rows // block)
        at = pl.ds(pl.multiple_of(b * block, block), block)
        amp_t[pl.ds(pl.multiple_of(r * cols, cols), cols), at] = amp[r, at, :].T

    shift_vir.wait_recv()

    occs, virs = occ.shape[1], vir.shape[1]
    share = virs // nv

    def split(value, by):
        by = jnp.full_like(value, by)
        return lax.div(value, by), lax.rem(value, by)

    def chosen(values, index):
        lane = lax.broadcasted_iota(jnp.int32, (block, values.shape[1]), 1)
        return jnp.sum(jnp.where(lane == index, values, 0.0), axis=1, keepdims=True)

    @pl.loop(0, rows // block)
    def _(b):
        row = b * block + lax.broadcasted_iota(jnp.int32, (block, 1), 0)
        if held.shape[1] > 1:
            i, a = split(row, virs)
        else:
            owner, rest = split(row, occs * share)
            i, a = split(rest, share)
            a += owner * share
        got = vir_got[...].astype(jnp.float32)[0:1, :]
        gap = chosen(got, a) - chosen(occ[...], i)
        at = pl.ds(pl.multiple_of(b * block, block), block)
        row_gap[at, :] = jnp.broadcast_to(gap, (block, row_gap.shape[1]))

    def spread(p):
        shift(p).wait_recv()
        for t in range(1, nx):
            gather_x(p, t).start()
        gather_core(p).start()

    def forward(p):
        for t in range(1, nx):
            gather_x(p, t).wait_recv()
            gather_forward(p, t).start()

    def energies(r):
        @pl.loop(0, rows // block)
        def _(b):
            at = pl.ds(pl.multiple_of(b * block, block), block)
            gap = row_gap[at, :]
            for h in range(0, cols, 128):
                acc[r, at, h:h + 128] = (gap + col_gap[:, h:h + 128]) * amp[r, at, h:h + 128].astype(jnp.float32)

    def cycle(p):
        gather_core(p).wait_recv()
        for t in range(1, nx):
            gather_forward(p, t).wait_recv()

        @pl.loop(0, 2)
        def _(i):
            at = pl.ds(pl.multiple_of(i * (total // 2), total // 2), total // 2)
            dot = jnp.dot(amp_t[at, :], held[p].reshape(rows, width), preferred_element_type=jnp.float32)
            part[p, at, :] = dot.astype(part.dtype)
        scatter(p, 0).start()

    def reduce(p, l):
        scatter(p, l).wait_recv()
        last = l == levels - 1
        into = full if last else part

        @pl.loop(0, (total >> (l + 1)) // piece)
        def _(i):
            at = pl.ds(pl.multiple_of(offset[l + 1] + i * piece, piece), piece)
            new = pl.ds(pl.multiple_of(total - (total >> l) + i * piece, piece), piece)
            both = part[p, at, :].astype(jnp.float32) + came[p, new, :].astype(jnp.float32)
            into[p, at, :] = both.astype(part.dtype)
        if last:
            gather(p, l).start()
        else:
            scatter(p, l + 1).start()

    def regather(p, l):
        gather(p, l).wait_recv()
        gather(p, l - 1).start()

    def deliver(r):
        return pltpu.make_async_copy(amp.at[r], out.at[r], out_sem.at[r])

    def sigma(p):
        gather(p, 0).wait_recv()

        def product(r):
            at = pl.ds(pl.multiple_of(r * cols, cols), cols)
            left = jnp.concatenate([held[p - 1].reshape(rows, width), held[p].reshape(rows, width)], axis=1)
            right = jnp.concatenate([full[p - 1, at, :], full[p, at, :]], axis=1)
            return lax.dot_general(
                left, right, (((1,), (1,)), ((), ())), preferred_element_type=jnp.float32)

        @pl.when((p < n - 1) & (lax.rem(p, 2) == 1))
        def _():
            @pl.loop(0, roots)
            def _(r):
                acc[r] += product(r)

        @pl.when(p == n - 1)
        def _():
            @pl.loop(0, roots)
            def _(r):
                amp[r] = (acc[r] + product(r)).astype(amp.dtype)
                deliver(r).start()

    stages, late = [(1, forward), (0, spread)], [(2, cycle)]
    delay = 2
    for l in range(levels):
        delay += 2
        stages.append((delay, functools.partial(reduce, l=l)))
    for l in range(levels - 1, 0, -1):
        delay += 2
        stages.append((delay, functools.partial(regather, l=l)))
    delay += 2
    late.append((delay, sigma))

    def step(s, carry):
        for i in range(2):
            later = 2 * s + AHEAD + i

            @pl.when(later < n)
            def _():
                shift(later).start()

        for behind_by, stage in stages + late:
            p = s - behind_by

            @pl.when((p >= 0) & (p < n))
            def _():
                stage(p)

        @pl.when(s < roots)
        def _():
            energies(s)

        return carry

    lax.fori_loop(0, n + delay, step, 0)

    def drain(p, carry):
        shift(p).wait_send()
        for t in range(1, nx):
            gather_x(p, t).wait_send()
            gather_forward(p, t).wait_send()
        gather_core(p).wait_send()
        for l in range(levels):
            scatter(p, l).wait_send()
            gather(p, l).wait_send()
        return carry

    lax.fori_loop(0, n, drain, 0)
    shift_vir.wait_send()
    for r in range(roots):
        deliver(r).wait()


def combine(distance, nk, nv, fac, vir, amp, occ, col_gap):
    outer, inner, aux = fac.shape
    roots, rows, cols = amp.shape
    width = 128
    n = aux // width
    nx, levels = nv // 2, (nk - 1).bit_length()
    total = roots * cols
    dma = pltpu.SemaphoreType.DMA
    vmem = pl.BlockSpec(memory_space=pltpu.VMEM)
    anywhere = pl.BlockSpec(memory_space=pl.ANY)
    bf = jnp.bfloat16
    return pl.pallas_call(
        functools.partial(kernel, nk, nv, n, distance),
        out_shape=jax.ShapeDtypeStruct((roots, rows, cols), bf),
        in_specs=[anywhere, vmem, anywhere, vmem, vmem],
        out_specs=anywhere,
        scratch_shapes=[
            pltpu.VMEM((n, outer, nv, inner, width), bf),
            pltpu.VMEM((16, vir.shape[1]), bf),
            pltpu.VMEM((16, vir.shape[1]), bf),
            pltpu.VMEM((rows, 128), jnp.float32),
            pltpu.VMEM((roots, rows, cols), bf),
            pltpu.VMEM((total, rows), bf),
            pltpu.VMEM((roots, rows, cols), jnp.float32),
            pltpu.VMEM((n, total, width), bf),
            pltpu.VMEM((n, total, width), bf),
            pltpu.VMEM((n, total, width), bf),
            dma, dma((roots,)), dma, dma,
            dma((n,)), dma((n,)),
            dma((n, nx - 1)), dma((n, nx - 1)),
            dma((n,)), dma((n,)),
            dma((n, nx - 1)), dma((n, nx - 1)),
            dma((n, levels)), dma((n, levels)),
            dma((n, levels)), dma((n, levels)),
        ],
        compiler_params=pltpu.CompilerParams(
            collective_id=distance, has_side_effects=True, vmem_limit_bytes=60 * 1024 * 1024),
        cost_estimate=pl.CostEstimate(
            flops=4 * roots * rows * cols * aux,
            bytes_accessed=4 * roots * rows * cols + 2 * outer * inner * aux,
            transcendentals=0),
    )(fac, vir, amp, occ, col_gap)


def shards(factors, amps, eps_occ, eps_vir, col_energy, q_index):
    nk, nv = lax.axis_size("kocc"), lax.axis_size("vrow")
    fac = factors[0]
    occ, share, aux = fac.shape
    amp = amps[:, 0]
    roots, _, vir, cols = amp.shape
    natural = share % 16 == 0
    if not natural:
        fac = fac.reshape(1, occ * share, aux)
        amp = amp.reshape(roots, occ, nv, share, cols).swapaxes(1, 2)
    operands = (fac, eps_vir, amp.reshape(roots, occ * vir, cols), eps_occ, col_energy[None, :])
    out = lax.switch(
        q_index[0] - 1, [functools.partial(combine, d, nk, nv) for d in range(1, nk)], *operands)
    if not natural:
        out = out.reshape(roots, nv, occ, share, cols).swapaxes(1, 2)
    return out.reshape(roots, 1, occ, vir, cols)


def solution(mesh):
    in_specs = (
        P("kocc", None, "vrow", None),
        P(None, "kocc", None, None, "vrow"),
        P("kocc", None),
        P("kocc", None),
        P("vrow"),
        P(),
    )
    out_specs = P(None, "kocc", None, None, "vrow")
    return jax.shard_map(shards, mesh=mesh, in_specs=in_specs, out_specs=out_specs, check_vma=False)
```

```python
import functools

import jax
import jax.numpy as jnp
from jax import lax
from jax.experimental import pallas as pl
from jax.experimental.pallas import tpu as pltpu
from jax.sharding import PartitionSpec as P

MESH = pl.DeviceIdType.MESH
AHEAD = 3


def kernel(nk, nv, n, distance, fac, vir, amp_in, occ, col_gap, out,
           held, vir_put, vir_got, row_gap, amp, amp_t, acc, part, came, full,
           amp_sem, out_sem, vir_s, vir_r, sh_s, sh_r, gx_s, gx_r, gc_s, gc_r, gf_s, gf_r,
           rs_s, rs_r, ag_s, ag_r):
    nx, levels = nv // 2, (nk - 1).bit_length()
    k, v = lax.axis_index("kocc"), lax.axis_index("vrow")
    core, x = lax.rem(v, 2), v // 2
    width = held.shape[-1]
    roots, rows, cols = amp.shape
    total = part.shape[1]
    piece = total // nk

    def at_vrow(target):
        return {"kocc": k, "vrow": target}

    def at_kocc(target):
        return {"kocc": target, "vrow": v}

    bit = [lax.rem(k // (1 << l), 2) for l in range(levels)]
    partner = [at_kocc(k + (1 - 2 * bit[l]) * (1 << l)) for l in range(levels)]
    offset = [0]
    for l in range(levels):
        offset.append(offset[-1] + bit[l] * (total >> (l + 1)))
    mate = at_vrow(x * 2 + 1 - core)
    ahead = at_kocc(lax.rem(k + distance, nk))
    behind = at_kocc(lax.rem(k + nk - distance, nk))

    def x_to(t):
        return lax.rem(x + t, nx)

    def x_from(t):
        return lax.rem(x + nx - t, nx)

    copy = pltpu.make_async_copy(amp_in, amp, amp_sem)
    copy.start()

    barrier = pltpu.get_barrier_semaphore()
    partners = [ahead, behind, mate] + partner
    partners += [at_vrow(x_to(t) * 2 + core) for t in range(1, nx)]
    for device in partners:
        pl.semaphore_signal(barrier, inc=1, device_id=device, device_id_type=MESH)
    pl.semaphore_wait(barrier, len(partners))

    def remote(src, dst, send, recv, device):
        return pltpu.make_async_remote_copy(
            src_ref=src, dst_ref=dst, send_sem=send, recv_sem=recv,
            device_id=device, device_id_type=MESH)

    def shift(p):
        return remote(fac.at[:, :, pl.ds(pl.multiple_of(p * width, width), width)],
                      held.at[p, :, v], sh_s.at[p], sh_r.at[p], ahead)

    def gather_x(p, t):
        return remote(held.at[p, :, v], held.at[p, :, v], gx_s.at[p, t - 1], gx_r.at[p, t - 1],
                      at_vrow(x_to(t) * 2 + core))

    def gather_core(p):
        return remote(held.at[p, :, v], held.at[p, :, v], gc_s.at[p], gc_r.at[p], mate)

    def gather_forward(p, t):
        slot = held.at[p, :, x_from(t) * 2 + core]
        return remote(slot, slot, gf_s.at[p, t - 1], gf_r.at[p, t - 1], mate)

    def scatter(p, l):
        size = total >> (l + 1)
        return remote(part.at[p, pl.ds(pl.multiple_of(offset[l] + (1 - bit[l]) * size, piece), size)],
                      came.at[p, pl.ds(total - (total >> l), size)],
                      rs_s.at[p, l], rs_r.at[p, l], partner[l])

    def gather(p, l):
        where = pl.ds(pl.multiple_of(offset[l + 1], piece), total >> (l + 1))
        return remote(full.at[p, where], full.at[p, where],
                      ag_s.at[p, l], ag_r.at[p, l], partner[l])

    for p in range(AHEAD):
        shift(p).start()
    vir_put[...] = jnp.broadcast_to(vir[...].astype(jnp.float32), vir_put.shape).astype(vir_put.dtype)
    shift_vir = remote(vir_put, vir_got, vir_s, vir_r, ahead)
    shift_vir.start()

    block = 256
    copy.wait()

    @pl.loop(0, roots * (rows // block))
    def _(i):
        r, b = i // (rows // block), lax.rem(i, rows // block)
        at = pl.ds(pl.multiple_of(b * block, block), block)
        amp_t[pl.ds(pl.multiple_of(r * cols, cols), cols), at] = amp[r, at, :].T

    shift_vir.wait_recv()

    occs, virs = occ.shape[1], vir.shape[1]
    share = virs // nv

    def split(value, by):
        by = jnp.full_like(value, by)
        return lax.div(value, by), lax.rem(value, by)

    def chosen(values, index):
        lane = lax.broadcasted_iota(jnp.int32, (block, values.shape[1]), 1)
        return jnp.sum(jnp.where(lane == index, values, 0.0), axis=1, keepdims=True)

    @pl.loop(0, rows // block)
    def _(b):
        row = b * block + lax.broadcasted_iota(jnp.int32, (block, 1), 0)
        if held.shape[1] > 1:
            i, a = split(row, virs)
        else:
            owner, rest = split(row, occs * share)
            i, a = split(rest, share)
            a += owner * share
        got = vir_got[...].astype(jnp.float32)[0:1, :]
        gap = chosen(got, a) - chosen(occ[...], i)
        at = pl.ds(pl.multiple_of(b * block, block), block)
        row_gap[at, :] = jnp.broadcast_to(gap, (block, row_gap.shape[1]))

    def spread(p):
        shift(p).wait_recv()
        for t in range(1, nx):
            gather_x(p, t).start()
        gather_core(p).start()

    def forward(p):
        for t in range(1, nx):
            gather_x(p, t).wait_recv()
            gather_forward(p, t).start()

    def energies(r):
        @pl.loop(0, rows // block)
        def _(b):
            at = pl.ds(pl.multiple_of(b * block, block), block)
            gap = row_gap[at, :]
            for h in range(0, cols, 128):
                acc[r, at, h:h + 128] = (gap + col_gap[:, h:h + 128]) * amp[r, at, h:h + 128].astype(jnp.float32)

    def cycle(p):
        gather_core(p).wait_recv()
        for t in range(1, nx):
            gather_forward(p, t).wait_recv()

        @pl.loop(0, 2)
        def _(i):
            at = pl.ds(pl.multiple_of(i * (total // 2), total // 2), total // 2)
            dot = jnp.dot(amp_t[at, :], held[p].reshape(rows, width), preferred_element_type=jnp.float32)
            part[p, at, :] = dot.astype(part.dtype)
        scatter(p, 0).start()

    def reduce(p, l):
        scatter(p, l).wait_recv()
        last = l == levels - 1
        into = full if last else part

        @pl.loop(0, (total >> (l + 1)) // piece)
        def _(i):
            at = pl.ds(pl.multiple_of(offset[l + 1] + i * piece, piece), piece)
            new = pl.ds(pl.multiple_of(total - (total >> l) + i * piece, piece), piece)
            both = part[p, at, :].astype(jnp.float32) + came[p, new, :].astype(jnp.float32)
            into[p, at, :] = both.astype(part.dtype)
        if last:
            gather(p, l).start()
        else:
            scatter(p, l + 1).start()

    def regather(p, l):
        gather(p, l).wait_recv()
        gather(p, l - 1).start()

    def deliver(r):
        return pltpu.make_async_copy(amp.at[r], out.at[r], out_sem.at[r])

    def sigma(p):
        gather(p, 0).wait_recv()

        def product(r):
            at = pl.ds(pl.multiple_of(r * cols, cols), cols)
            left = jnp.concatenate([held[p - 1].reshape(rows, width), held[p].reshape(rows, width)], axis=1)
            right = jnp.concatenate([full[p - 1, at, :], full[p, at, :]], axis=1)
            return lax.dot_general(
                left, right, (((1,), (1,)), ((), ())), preferred_element_type=jnp.float32)

        @pl.when((p < n - 1) & (lax.rem(p, 2) == 1))
        def _():
            @pl.loop(0, roots)
            def _(r):
                acc[r] += product(r)

        @pl.when(p == n - 1)
        def _():
            @pl.loop(0, roots)
            def _(r):
                amp[r] = (acc[r] + product(r)).astype(amp.dtype)
                deliver(r).start()

    stages, late = [(1, forward), (0, spread)], [(2, cycle)]
    delay = 2
    for l in range(levels):
        delay += 2 if l == 0 else 1
        stages.append((delay, functools.partial(reduce, l=l)))
    for l in range(levels - 1, 0, -1):
        delay += 1
        stages.append((delay, functools.partial(regather, l=l)))
    delay += 2
    late.append((delay, sigma))

    def step(s, carry):
        @pl.when(s + AHEAD < n)
        def _():
            shift(s + AHEAD).start()

        for behind_by, stage in stages + late:
            p = s - behind_by

            @pl.when((p >= 0) & (p < n))
            def _():
                stage(p)

        @pl.when(s < roots)
        def _():
            energies(s)

        return carry

    lax.fori_loop(0, n + delay, step, 0)

    def drain(p, carry):
        shift(p).wait_send()
        for t in range(1, nx):
            gather_x(p, t).wait_send()
            gather_forward(p, t).wait_send()
        gather_core(p).wait_send()
        for l in range(levels):
            scatter(p, l).wait_send()
            gather(p, l).wait_send()
        return carry

    lax.fori_loop(0, n, drain, 0)
    shift_vir.wait_send()
    for r in range(roots):
        deliver(r).wait()


def combine(distance, nk, nv, fac, vir, amp, occ, col_gap):
    outer, inner, aux = fac.shape
    roots, rows, cols = amp.shape
    width = 128
    n = aux // width
    nx, levels = nv // 2, (nk - 1).bit_length()
    total = roots * cols
    dma = pltpu.SemaphoreType.DMA
    vmem = pl.BlockSpec(memory_space=pltpu.VMEM)
    anywhere = pl.BlockSpec(memory_space=pl.ANY)
    bf = jnp.bfloat16
    return pl.pallas_call(
        functools.partial(kernel, nk, nv, n, distance),
        out_shape=jax.ShapeDtypeStruct((roots, rows, cols), bf),
        in_specs=[anywhere, vmem, anywhere, vmem, vmem],
        out_specs=anywhere,
        scratch_shapes=[
            pltpu.VMEM((n, outer, nv, inner, width), bf),
            pltpu.VMEM((16, vir.shape[1]), bf),
            pltpu.VMEM((16, vir.shape[1]), bf),
            pltpu.VMEM((rows, 128), jnp.float32),
            pltpu.VMEM((roots, rows, cols), bf),
            pltpu.VMEM((total, rows), bf),
            pltpu.VMEM((roots, rows, cols), jnp.float32),
            pltpu.VMEM((n, total, width), bf),
            pltpu.VMEM((n, total, width), bf),
            pltpu.VMEM((n, total, width), bf),
            dma, dma((roots,)), dma, dma,
            dma((n,)), dma((n,)),
            dma((n, nx - 1)), dma((n, nx - 1)),
            dma((n,)), dma((n,)),
            dma((n, nx - 1)), dma((n, nx - 1)),
            dma((n, levels)), dma((n, levels)),
            dma((n, levels)), dma((n, levels)),
        ],
        compiler_params=pltpu.CompilerParams(
            collective_id=distance, has_side_effects=True, vmem_limit_bytes=60 * 1024 * 1024),
        cost_estimate=pl.CostEstimate(
            flops=4 * roots * rows * cols * aux,
            bytes_accessed=4 * roots * rows * cols + 2 * outer * inner * aux,
            transcendentals=0),
    )(fac, vir, amp, occ, col_gap)


def shards(factors, amps, eps_occ, eps_vir, col_energy, q_index):
    nk, nv = lax.axis_size("kocc"), lax.axis_size("vrow")
    fac = factors[0]
    occ, share, aux = fac.shape
    amp = amps[:, 0]
    roots, _, vir, cols = amp.shape
    natural = share % 16 == 0
    if not natural:
        fac = fac.reshape(1, occ * share, aux)
        amp = amp.reshape(roots, occ, nv, share, cols).swapaxes(1, 2)
    operands = (fac, eps_vir, amp.reshape(roots, occ * vir, cols), eps_occ, col_energy[None, :])
    out = lax.switch(
        q_index[0] - 1, [functools.partial(combine, d, nk, nv) for d in range(1, nk)], *operands)
    if not natural:
        out = out.reshape(roots, nv, occ, share, cols).swapaxes(1, 2)
    return out.reshape(roots, 1, occ, vir, cols)


def solution(mesh):
    in_specs = (
        P("kocc", None, "vrow", None),
        P(None, "kocc", None, None, "vrow"),
        P("kocc", None),
        P("kocc", None),
        P("vrow"),
        P(),
    )
    out_specs = P(None, "kocc", None, None, "vrow")
    return jax.shard_map(shards, mesh=mesh, in_specs=in_specs, out_specs=out_specs, check_vma=False)
```

```python
import functools

import jax
import jax.numpy as jnp
from jax import lax
from jax.experimental import pallas as pl
from jax.experimental.pallas import tpu as pltpu
from jax.sharding import PartitionSpec as P

MESH = pl.DeviceIdType.MESH
AHEAD = 3


def kernel(nk, nv, n, distance, fac, vir, amp_in, occ, col_gap, out,
           held, vir_put, vir_got, row_gap, amp, amp_t, acc, part, came, full,
           amp_sem, out_sem, vir_s, vir_r, sh_s, sh_r, gx_s, gx_r, gc_s, gc_r, gf_s, gf_r,
           rs_s, rs_r, ag_s, ag_r):
    nx, levels = nv // 2, (nk - 1).bit_length()
    k, v = lax.axis_index("kocc"), lax.axis_index("vrow")
    core, x = lax.rem(v, 2), v // 2
    width = held.shape[-1]
    roots, rows, cols = amp.shape
    total = part.shape[1]
    piece = total // nk

    def at_vrow(target):
        return {"kocc": k, "vrow": target}

    def at_kocc(target):
        return {"kocc": target, "vrow": v}

    bit = [lax.rem(k // (1 << l), 2) for l in range(levels)]
    partner = [at_kocc(k + (1 - 2 * bit[l]) * (1 << l)) for l in range(levels)]
    offset = [0]
    for l in range(levels):
        offset.append(offset[-1] + bit[l] * (total >> (l + 1)))
    mate = at_vrow(x * 2 + 1 - core)
    ahead = at_kocc(lax.rem(k + distance, nk))
    behind = at_kocc(lax.rem(k + nk - distance, nk))

    def x_to(t):
        return lax.rem(x + t, nx)

    def x_from(t):
        return lax.rem(x + nx - t, nx)

    copy = pltpu.make_async_copy(amp_in, amp, amp_sem)
    copy.start()

    barrier = pltpu.get_barrier_semaphore()
    partners = [ahead, behind, mate] + partner
    partners += [at_vrow(x_to(t) * 2 + core) for t in range(1, nx)]
    for device in partners:
        pl.semaphore_signal(barrier, inc=1, device_id=device, device_id_type=MESH)
    pl.semaphore_wait(barrier, len(partners))

    def remote(src, dst, send, recv, device):
        return pltpu.make_async_remote_copy(
            src_ref=src, dst_ref=dst, send_sem=send, recv_sem=recv,
            device_id=device, device_id_type=MESH)

    def shift(p):
        return remote(fac.at[:, :, pl.ds(pl.multiple_of(p * width, width), width)],
                      held.at[p, :, v], sh_s.at[p], sh_r.at[p], ahead)

    def gather_x(p, t):
        return remote(held.at[p, :, v], held.at[p, :, v], gx_s.at[p, t - 1], gx_r.at[p, t - 1],
                      at_vrow(x_to(t) * 2 + core))

    def gather_core(p):
        return remote(held.at[p, :, v], held.at[p, :, v], gc_s.at[p], gc_r.at[p], mate)

    def gather_forward(p, t):
        slot = held.at[p, :, x_from(t) * 2 + core]
        return remote(slot, slot, gf_s.at[p, t - 1], gf_r.at[p, t - 1], mate)

    def scatter(p, l):
        if l < levels - 1:
            size = total >> (l + 1)
            start = offset[l] + (1 - bit[l]) * size
        else:
            size = total >> l
            start = offset[l]
        return remote(part.at[p, pl.ds(pl.multiple_of(start, piece), size)],
                      came.at[p, pl.ds(total - (total >> l), size)],
                      rs_s.at[p, l], rs_r.at[p, l], partner[l])

    def gather(p, l):
        where = pl.ds(pl.multiple_of(offset[l + 1], piece), total >> (l + 1))
        return remote(full.at[p, where], full.at[p, where],
                      ag_s.at[p, l], ag_r.at[p, l], partner[l])

    for p in range(AHEAD):
        shift(p).start()
    vir_put[...] = jnp.broadcast_to(vir[...].astype(jnp.float32), vir_put.shape).astype(vir_put.dtype)
    shift_vir = remote(vir_put, vir_got, vir_s, vir_r, ahead)
    shift_vir.start()

    block = 256
    copy.wait()

    @pl.loop(0, roots * (rows // block))
    def _(i):
        r, b = i // (rows // block), lax.rem(i, rows // block)
        at = pl.ds(pl.multiple_of(b * block, block), block)
        amp_t[pl.ds(pl.multiple_of(r * cols, cols), cols), at] = amp[r, at, :].T

    shift_vir.wait_recv()

    occs, virs = occ.shape[1], vir.shape[1]
    share = virs // nv

    def split(value, by):
        by = jnp.full_like(value, by)
        return lax.div(value, by), lax.rem(value, by)

    def chosen(values, index):
        lane = lax.broadcasted_iota(jnp.int32, (block, values.shape[1]), 1)
        return jnp.sum(jnp.where(lane == index, values, 0.0), axis=1, keepdims=True)

    @pl.loop(0, rows // block)
    def _(b):
        row = b * block + lax.broadcasted_iota(jnp.int32, (block, 1), 0)
        if held.shape[1] > 1:
            i, a = split(row, virs)
        else:
            owner, rest = split(row, occs * share)
            i, a = split(rest, share)
            a += owner * share
        got = vir_got[...].astype(jnp.float32)[0:1, :]
        gap = chosen(got, a) - chosen(occ[...], i)
        at = pl.ds(pl.multiple_of(b * block, block), block)
        row_gap[at, :] = jnp.broadcast_to(gap, (block, row_gap.shape[1]))

    def spread(p):
        shift(p).wait_recv()
        for t in range(1, nx):
            gather_x(p, t).start()
        gather_core(p).start()

    def forward(p):
        for t in range(1, nx):
            gather_x(p, t).wait_recv()
            gather_forward(p, t).start()

    def energies(r):
        @pl.loop(0, rows // block)
        def _(b):
            at = pl.ds(pl.multiple_of(b * block, block), block)
            gap = row_gap[at, :]
            for h in range(0, cols, 128):
                acc[r, at, h:h + 128] = (gap + col_gap[:, h:h + 128]) * amp[r, at, h:h + 128].astype(jnp.float32)

    def cycle(p):
        gather_core(p).wait_recv()
        for t in range(1, nx):
            gather_forward(p, t).wait_recv()

        @pl.loop(0, 2)
        def _(i):
            at = pl.ds(pl.multiple_of(i * (total // 2), total // 2), total // 2)
            dot = jnp.dot(amp_t[at, :], held[p].reshape(rows, width), preferred_element_type=jnp.float32)
            part[p, at, :] = dot.astype(part.dtype)
        scatter(p, 0).start()

    def reduce(p, l):
        scatter(p, l).wait_recv()
        last = l == levels - 1
        into = full if last else part
        kept = l if last else l + 1

        @pl.loop(0, (total >> kept) // piece)
        def _(i):
            at = pl.ds(pl.multiple_of(offset[kept] + i * piece, piece), piece)
            new = pl.ds(pl.multiple_of(total - (total >> l) + i * piece, piece), piece)
            both = part[p, at, :].astype(jnp.float32) + came[p, new, :].astype(jnp.float32)
            into[p, at, :] = both.astype(part.dtype)
        if last:
            gather(p, l - 1).start()
        else:
            scatter(p, l + 1).start()

    def regather(p, l):
        gather(p, l).wait_recv()
        gather(p, l - 1).start()

    def deliver(r):
        return pltpu.make_async_copy(amp.at[r], out.at[r], out_sem.at[r])

    def sigma(p):
        gather(p, 0).wait_recv()

        def product(r):
            at = pl.ds(pl.multiple_of(r * cols, cols), cols)
            left = jnp.concatenate([held[p - 1].reshape(rows, width), held[p].reshape(rows, width)], axis=1)
            right = jnp.concatenate([full[p - 1, at, :], full[p, at, :]], axis=1)
            return lax.dot_general(
                left, right, (((1,), (1,)), ((), ())), preferred_element_type=jnp.float32)

        @pl.when((p < n - 1) & (lax.rem(p, 2) == 1))
        def _():
            @pl.loop(0, roots)
            def _(r):
                acc[r] += product(r)

        @pl.when(p == n - 1)
        def _():
            @pl.loop(0, roots)
            def _(r):
                amp[r] = (acc[r] + product(r)).astype(amp.dtype)
                deliver(r).start()

    stages = [(2, cycle), (1, forward), (0, spread)]
    stages += [(3 + l, functools.partial(reduce, l=l)) for l in range(levels)]
    delay = 2 + levels
    for l in range(levels - 2, 0, -1):
        delay += 1
        stages.append((delay, functools.partial(regather, l=l)))
    delay += 1
    stages.append((delay, sigma))

    def step(s, carry):
        @pl.when(s + AHEAD < n)
        def _():
            shift(s + AHEAD).start()

        for behind_by, stage in stages:
            p = s - behind_by

            @pl.when((p >= 0) & (p < n))
            def _():
                stage(p)

        @pl.when(s < roots)
        def _():
            energies(s)

        return carry

    lax.fori_loop(0, n + delay, step, 0)

    def drain(p, carry):
        shift(p).wait_send()
        for t in range(1, nx):
            gather_x(p, t).wait_send()
            gather_forward(p, t).wait_send()
        gather_core(p).wait_send()
        for l in range(levels):
            scatter(p, l).wait_send()
        for l in range(levels - 1):
            gather(p, l).wait_send()
        return carry

    lax.fori_loop(0, n, drain, 0)
    shift_vir.wait_send()
    for r in range(roots):
        deliver(r).wait()


def combine(distance, nk, nv, fac, vir, amp, occ, col_gap):
    outer, inner, aux = fac.shape
    roots, rows, cols = amp.shape
    width = 128
    n = aux // width
    nx, levels = nv // 2, (nk - 1).bit_length()
    total = roots * cols
    dma = pltpu.SemaphoreType.DMA
    vmem = pl.BlockSpec(memory_space=pltpu.VMEM)
    anywhere = pl.BlockSpec(memory_space=pl.ANY)
    bf = jnp.bfloat16
    return pl.pallas_call(
        functools.partial(kernel, nk, nv, n, distance),
        out_shape=jax.ShapeDtypeStruct((roots, rows, cols), bf),
        in_specs=[anywhere, vmem, anywhere, vmem, vmem],
        out_specs=anywhere,
        scratch_shapes=[
            pltpu.VMEM((n, outer, nv, inner, width), bf),
            pltpu.VMEM((16, vir.shape[1]), bf),
            pltpu.VMEM((16, vir.shape[1]), bf),
            pltpu.VMEM((rows, 128), jnp.float32),
            pltpu.VMEM((roots, rows, cols), bf),
            pltpu.VMEM((total, rows), bf),
            pltpu.VMEM((roots, rows, cols), jnp.float32),
            pltpu.VMEM((n, total, width), bf),
            pltpu.VMEM((n, total, width), bf),
            pltpu.VMEM((n, total, width), bf),
            dma, dma((roots,)), dma, dma,
            dma((n,)), dma((n,)),
            dma((n, nx - 1)), dma((n, nx - 1)),
            dma((n,)), dma((n,)),
            dma((n, nx - 1)), dma((n, nx - 1)),
            dma((n, levels)), dma((n, levels)),
            dma((n, levels - 1)), dma((n, levels - 1)),
        ],
        compiler_params=pltpu.CompilerParams(
            collective_id=distance, has_side_effects=True, vmem_limit_bytes=60 * 1024 * 1024),
        cost_estimate=pl.CostEstimate(
            flops=4 * roots * rows * cols * aux,
            bytes_accessed=4 * roots * rows * cols + 2 * outer * inner * aux,
            transcendentals=0),
    )(fac, vir, amp, occ, col_gap)


def shards(factors, amps, eps_occ, eps_vir, col_energy, q_index):
    nk, nv = lax.axis_size("kocc"), lax.axis_size("vrow")
    fac = factors[0]
    occ, share, aux = fac.shape
    amp = amps[:, 0]
    roots, _, vir, cols = amp.shape
    natural = share % 16 == 0
    if not natural:
        fac = fac.reshape(1, occ * share, aux)
        amp = amp.reshape(roots, occ, nv, share, cols).swapaxes(1, 2)
    operands = (fac, eps_vir, amp.reshape(roots, occ * vir, cols), eps_occ, col_energy[None, :])
    out = lax.switch(
        q_index[0] - 1, [functools.partial(combine, d, nk, nv) for d in range(1, nk)], *operands)
    if not natural:
        out = out.reshape(roots, nv, occ, share, cols).swapaxes(1, 2)
    return out.reshape(roots, 1, occ, vir, cols)


def solution(mesh):
    in_specs = (
        P("kocc", None, "vrow", None),
        P(None, "kocc", None, None, "vrow"),
        P("kocc", None),
        P("kocc", None),
        P("vrow"),
        P(),
    )
    out_specs = P(None, "kocc", None, None, "vrow")
    return jax.shard_map(shards, mesh=mesh, in_specs=in_specs, out_specs=out_specs, check_vma=False)
```
